128 devices in a mesh: grp: 8 (over z, core), sp: 16 (over x, y).
Axes of the slice: x: 4, y: 4, z: 4, core: 2. Of those that a mesh axis runs over, the one named last changes fastest.
Arguments:
- queries: bfloat16 [16, 16, 256, 1536], P(None, None, ('grp', 'sp')), may hold values from -64 to 64
- key_rows: bfloat16 [16, 16, 256, 1536], P(None, None, ('grp', 'sp')), may hold values from -6 to 6
- values: bfloat16 [16, 16, 256, 1536], P(None, None, ('grp', 'sp')), may hold values from -6 to 6
- query_gain: float32 [128], replicated, may hold values from 0.3 to 4.5
- key_gain: float32 [128], replicated, may hold values from 0.3 to 4.5
- frames_per_clip: int32 [16], replicated, may hold values from 4 to 16, as said below
- latent_height: int32 [16], replicated, may hold values from 2 to 4, as said below
- latent_width: int32 [16], replicated, may hold values from 32 to 64, as said below
- clip_plan: int32 [8], replicated, may hold values from 0 to 15, as said below
Outputs:
- block_out: bfloat16 [8, 16, 256, 1536], P('grp', 'sp')
The draws below stay inside these ranges and needn't reach their ends.
Inputs may be any that keep to these rules, and one draw needn't show every extreme that they name: `frames_per_clip`: at least a quarter of 16; some clip named by clip_plan has exactly 16 frames and also the largest height and width. `latent_height`: some clip named by clip_plan reaches 4. `latent_width`: some clip named by clip_plan reaches 64. `clip_plan`: distinct clips, one for each group.
All inputs are finite; a program needn't handle non-finite values.
Results may differ from the reference program's by a relative error of at most 0.0054.
Values may be sent and summed in bfloat16 or wider, within the bound.
A program may use at most 64 MiB of HBM per device.

```python
import jax
import jax.numpy as jnp
from jax import lax

HEADS = 12
HEAD_DIM = 128
HMAX = 4
WMAX = 64
SMAX = 256
FMAX = 16
GROUPS = 8
CLIPS = 16


def frame_likeness(key, apart_low, apart_high):
    spread = jax.random.uniform(jax.random.fold_in(key, 301), (CLIPS, 1, SMAX, 1), jnp.float32)
    log_low = jnp.log(jnp.float32(apart_low))
    log_high = jnp.log(jnp.float32(apart_high))
    return 1.0 - jnp.exp(log_low + spread * (log_high - log_low))


def frame_series(key, stream, likeness):
    shared = jax.random.normal(jax.random.fold_in(key, stream), (CLIPS, 1, SMAX, HEADS * HEAD_DIM), jnp.float32)
    per_frame = jax.random.normal(jax.random.fold_in(key, stream + 1), (CLIPS, FMAX, SMAX, HEADS * HEAD_DIM), jnp.float32)
    shared = jnp.clip(shared, -6.0, 6.0)
    per_frame = jnp.clip(per_frame, -6.0, 6.0)
    return jnp.sqrt(likeness) * shared + jnp.sqrt(1.0 - likeness) * per_frame


def key_series(key, apart_low, apart_high):
    likeness = frame_likeness(key, apart_low, apart_high)
    return jnp.clip(frame_series(key, 101, likeness), -6.0, 6.0)


def group_plan(key):
    others = jax.random.permutation(jax.random.fold_in(key, 60), CLIPS - 1).astype(jnp.int32)
    slot = jax.random.randint(jax.random.fold_in(key, 61), (), 0, GROUPS)
    index = jnp.arange(GROUPS, dtype=jnp.int32)
    before = jnp.take(others, jnp.clip(index, 0, CLIPS - 2))
    after = jnp.take(others, jnp.clip(index - 1, 0, CLIPS - 2))
    result = jnp.where(index < slot, before, jnp.where(index == slot, CLIPS - 1, after))
    return result.astype(jnp.int32)


def biggest_clip(key):
    chosen = jax.random.randint(jax.random.fold_in(key, 77), (), 0, GROUPS)
    return group_plan(key)[chosen]


def draw_clip_plan(key, part):
    result = group_plan(key)
    return result


def draw_key_rows(key, part):
    result = key_series(key, 0.05, 0.4)
    return result.astype(jnp.bfloat16)


def draw_queries(key, part):
    base_key = key
    likeness = frame_likeness(base_key, 0.05, 0.4)
    key = jax.random.fold_in(key, 1)
    own_rows = 2.0 * frame_series(key, 11, likeness)
    result = own_rows
    return jnp.clip(result, -64.0, 64.0).astype(jnp.bfloat16)


def draw_values(key, part):
    likeness = frame_likeness(key, 0.05, 0.4)
    key = jax.random.fold_in(key, 10)
    result = frame_series(key, 21, likeness)
    return jnp.clip(result, -6.0, 6.0).astype(jnp.bfloat16)


def draw_query_gain(key, part):
    key = jax.random.fold_in(key, 3)
    result = jnp.exp(jax.random.uniform(key, (HEAD_DIM,), jnp.float32, -1.2, 0.0))
    return result


def draw_key_gain(key, part):
    key = jax.random.fold_in(key, 4)
    result = jnp.exp(jax.random.uniform(key, (HEAD_DIM,), jnp.float32, -1.2, 0.0))
    return result


def draw_frames_per_clip(key, part):
    largest = biggest_clip(key)
    key = jax.random.fold_in(key, 7)
    counts = jax.random.randint(key, (CLIPS,), max(1, FMAX // 4), FMAX + 1)
    return jnp.where(jnp.arange(CLIPS) == largest, FMAX, counts).astype(jnp.int32)


def draw_latent_height(key, part):
    largest = biggest_clip(key)
    key = jax.random.fold_in(key, 8)
    counts = jax.random.randint(key, (CLIPS,), max(1, HMAX // 2), HMAX + 1)
    return jnp.where(jnp.arange(CLIPS) == largest, HMAX, counts).astype(jnp.int32)


def draw_latent_width(key, part):
    largest = biggest_clip(key)
    key = jax.random.fold_in(key, 9)
    counts = jax.random.randint(key, (CLIPS,), max(1, WMAX // 2), WMAX + 1)
    return jnp.where(jnp.arange(CLIPS) == largest, WMAX, counts).astype(jnp.int32)


def setup_inputs(seed: int = 0) -> dict:
    key_list = jax.random.split(jax.random.key(seed), 10)
    queries = draw_queries(jax.random.fold_in(key_list[9], 71), 0)
    key_rows = draw_key_rows(jax.random.fold_in(key_list[9], 71), 0)
    values = draw_values(jax.random.fold_in(key_list[9], 71), 0)
    query_gain = draw_query_gain(jax.random.fold_in(key_list[9], 71), 0)
    key_gain = draw_key_gain(jax.random.fold_in(key_list[9], 71), 0)
    frames_per_clip = draw_frames_per_clip(jax.random.fold_in(key_list[9], 71), 0)
    latent_height = draw_latent_height(jax.random.fold_in(key_list[9], 71), 0)
    latent_width = draw_latent_width(jax.random.fold_in(key_list[9], 71), 0)
    clip_plan = draw_clip_plan(jax.random.fold_in(key_list[9], 71), 0)
    return dict(queries=queries, key_rows=key_rows, values=values, query_gain=query_gain, key_gain=key_gain, frames_per_clip=frames_per_clip, latent_height=latent_height, latent_width=latent_width, clip_plan=clip_plan)


def spatial_frame(query_frame, key_frame, value_frame, frame_number, frame_limit, live_count):
    head_count = query_frame.shape[1] // HEAD_DIM
    score_scale = HEAD_DIM ** (-0.5)
    query_heads = query_frame.reshape(SMAX, head_count, HEAD_DIM).astype(jnp.float32)
    key_heads = key_frame.reshape(SMAX, head_count, HEAD_DIM).astype(jnp.float32)
    value_heads = value_frame.reshape(SMAX, head_count, HEAD_DIM).astype(jnp.float32)
    scores = jnp.einsum('qhd,khd->hqk', query_heads, key_heads) * score_scale
    positions = jnp.arange(SMAX, dtype=jnp.int32)
    key_live = positions < live_count
    scores = jnp.where(key_live[None, None, :], scores, -jnp.inf)
    maxima = lax.optimization_barrier(jnp.max(scores, axis=-1, keepdims=True))
    weights = jnp.exp(scores - maxima)
    totals = lax.optimization_barrier(jnp.sum(weights, axis=-1))
    rounded = lax.optimization_barrier(weights.astype(jnp.bfloat16)).astype(jnp.float32)
    mixed = jnp.einsum('hqk,khd->qhd', rounded, value_heads) / jnp.transpose(totals)[:, :, None]
    rows_live = key_live & (frame_number < frame_limit)
    mixed = jnp.where(rows_live[:, None, None], mixed, jnp.float32(0.0))
    return mixed.reshape(SMAX, head_count * HEAD_DIM).astype(jnp.bfloat16)

def temporal_mix(arrived, query_gain, key_gain, frame_limit, live_count):
    score_scale = HEAD_DIM ** (-0.5)
    values32 = arrived.astype(jnp.float32)
    normed = values32 * lax.rsqrt(lax.optimization_barrier(jnp.mean(values32 * values32, axis=-1, keepdims=True)) + 1e-06)
    query_side = normed * query_gain
    key_side = normed * key_gain
    scores = jnp.einsum('fshd,gshd->shfg', query_side, key_side, precision=lax.Precision.HIGHEST) * score_scale
    frame_ids = jnp.arange(arrived.shape[0], dtype=jnp.int32)
    frames_live = frame_ids < frame_limit
    scores = jnp.where(frames_live[None, None, None, :], scores, -jnp.inf)
    maxima = lax.optimization_barrier(jnp.max(scores, axis=-1, keepdims=True))
    weights = jnp.exp(scores - maxima)
    totals = lax.optimization_barrier(jnp.sum(weights, axis=-1))
    rounded = lax.optimization_barrier(weights.astype(jnp.bfloat16)).astype(jnp.float32)
    mixed = jnp.einsum('shfg,gshd->fshd', rounded, values32, precision=lax.Precision.HIGHEST)
    mixed = mixed / jnp.transpose(totals, (2, 0, 1))[..., None]
    positions = jnp.arange(arrived.shape[1], dtype=jnp.int32)
    rows_live = frames_live[:, None] & (positions < live_count)[None, :]
    mixed = jnp.where(rows_live[:, :, None, None], mixed, jnp.float32(0.0))
    return mixed.astype(jnp.bfloat16)

def reference(queries, key_rows, values, query_gain, key_gain, frames_per_clip, latent_height, latent_width, clip_plan):
    row_width = HEADS * HEAD_DIM

    def per_group(group_number):
        current_clip = clip_plan[group_number]
        frame_limit = frames_per_clip[current_clip]
        live_count = latent_height[current_clip] * latent_width[current_clip]
        frame_ids = jnp.arange(FMAX, dtype=jnp.int32)

        def one_frame(packed):
            return spatial_frame(packed[0], packed[1], packed[2], packed[3], frame_limit, live_count)
        spatial = lax.map(one_frame, (queries[current_clip], key_rows[current_clip], values[current_clip], frame_ids))
        stacked = spatial.reshape(FMAX, SMAX, HEADS, HEAD_DIM)
        temporal = temporal_mix(stacked, query_gain, key_gain, frame_limit, live_count)
        summed = stacked.astype(jnp.float32) + temporal.astype(jnp.float32)
        return summed.astype(jnp.bfloat16).reshape(FMAX, SMAX, row_width)
    return lax.map(per_group, jnp.arange(GROUPS, dtype=jnp.int32))
```

```python
import functools
import math

import jax
import jax.numpy as jnp
from jax import lax
from jax.experimental import pallas as pl
from jax.experimental.pallas import tpu as pltpu
from jax.sharding import PartitionSpec as P

MESH = pl.DeviceIdType.MESH
D = 128
HEADS = 12
FRAMES = 16
POS = 256
DEVS = 128
CHUNKS = 2
FC = FRAMES // CHUNKS
PCHUNKS = 4
PC = POS // PCHUNKS
LOG2E = math.log2(math.e)
SCALE = D**-0.5


def idle_rank(z, c, x, y):
    return lax.rem(x + y + z - 2 * c + 8, 4)


def kernel(
    plan, frames, height, width, q_hbm, k_hbm, v_hbm, gq, gk, out,
    xq, xk, xv, stage, recv, spat, sendbuf,
    x_sem, in_send, in_recv, out_send, out_recv, ready,
):
    my_g = lax.axis_index("grp")
    my_s = lax.axis_index("sp")
    me = my_g * 16 + my_s
    mz, mc = lax.div(my_g, 2), lax.rem(my_g, 2)
    mx, my = lax.div(my_s, 4), lax.rem(my_s, 4)
    my_rank = idle_rank(mz, mc, mx, my)
    active = my_rank > 0
    my_head = jnp.maximum(mx * 3 + my_rank - 1, 0)

    barrier = pltpu.get_barrier_semaphore()

    def greet_grp(i, _):
        pl.semaphore_signal(barrier, 1, device_id=(lax.rem(my_g + i, 8), my_s), device_id_type=MESH)
        return 0

    def greet_sp(i, _):
        pl.semaphore_signal(barrier, 1, device_id=(my_g, lax.rem(my_s + i, 16)), device_id_type=MESH)
        return 0

    def greet_all(i, _):
        pl.semaphore_signal(ready, 1, device_id=(my_g, lax.rem(my_s + i, 16)), device_id_type=MESH)
        return 0

    lax.fori_loop(1, 8, greet_grp, 0)
    lax.fori_loop(1, 16, greet_sp, 0)
    loads = [
        pltpu.make_async_copy(ref, held, x_sem.at[t])
        for t, (ref, held) in enumerate(((q_hbm, xq), (k_hbm, xk), (v_hbm, xv)))
    ]
    for copy in loads:
        copy.start()
    pl.semaphore_wait(barrier, 22)
    lax.fori_loop(1, 16, greet_all, 0)

    stage_rows = stage.reshape(8, 3, FRAMES * HEADS * 2, D)
    for t, held in enumerate((xq, xk, xv)):
        loads[t].wait()
        x_rows = held.reshape(16, FRAMES * HEADS * 2, D)

        def pick(g, _):
            stage_rows[g, t] = x_rows[plan[g]]
            return 0

        lax.fori_loop(0, 8, pick, 0)
    pl.semaphore_wait(ready, 15)

    for ch in range(CHUNKS):
        span = pl.ds(ch * FC, FC)

        def send_unit(i, _):
            j = lax.rem(i * 45, 128)
            c = lax.rem(mc + lax.rem(j, 2), 2)
            z = lax.rem(mz + lax.rem(lax.div(j, 2), 4), 4)
            x = lax.rem(mx + lax.rem(lax.div(j, 8), 4), 4)
            y = lax.rem(my + lax.div(j, 32), 4)
            rank = idle_rank(z, c, x, y)
            g, s = z * 2 + c, x * 4 + y
            head = jnp.maximum(x * 3 + rank - 1, 0)
            src = stage.at[g, :, span, head]
            dst = recv.at[:, span, me]

            @pl.when((rank > 0) & (j != 0))
            def _():
                pltpu.make_async_remote_copy(
                    src, dst, in_send, in_recv.at[ch], device_id=(g, s), device_id_type=MESH
                ).start()

            @pl.when((rank > 0) & (j == 0))
            def _():
                pltpu.make_async_copy(src, dst, in_recv.at[ch]).start()

            return 0

        lax.fori_loop(0, 128, send_unit, 0)

    @pl.when(active)
    def _():
        clip = plan[my_g]
        live_frames = frames[clip]
        live_pos = height[clip] * width[clip]
        rows = recv.reshape(3, FRAMES, POS, D)
        key_ids = lax.broadcasted_iota(jnp.int32, (1, POS), 1)
        key_bias = jnp.where(key_ids < live_pos, 0.0, -jnp.inf).astype(jnp.float32)
        row_ids = lax.broadcasted_iota(jnp.int32, (POS, 1), 0)
        row_live = jnp.where(row_ids < live_pos, 1.0, 0.0).astype(jnp.float32)

        def spatial(f, _):
            scores = lax.dot_general(
                rows[0, f], rows[1, f], (((1,), (1,)), ((), ())), preferred_element_type=jnp.float32
            )
            scores = scores + key_bias
            top = jnp.max(scores, axis=-1, keepdims=True)
            weights = jnp.exp2((scores - top) * (SCALE * LOG2E))
            total = jnp.sum(weights, axis=-1, keepdims=True)
            mixed = jnp.dot(weights.astype(jnp.bfloat16), rows[2, f], preferred_element_type=jnp.float32)
            on = jnp.where(f < live_frames, 1.0, 0.0).astype(jnp.float32)
            mixed = (mixed / total) * (row_live * on)
            spat[f] = mixed.astype(jnp.bfloat16).astype(jnp.float32)
            return 0

        for ch in range(CHUNKS):
            part = recv.at[:, pl.ds(ch * FC, FC)]
            pltpu.make_async_copy(part, part, in_recv.at[ch]).wait()
            lax.fori_loop(ch * FC, (ch + 1) * FC, spatial, 0)

        gain = (gq[...] * gk[...]) * (SCALE * LOG2E)
        B = 8
        T = FRAMES * B
        r_id = lax.broadcasted_iota(jnp.int32, (T, T), 0)
        c_id = lax.broadcasted_iota(jnp.int32, (T, T), 1)
        pair_on = (lax.rem(r_id, B) == lax.rem(c_id, B)) & (lax.div(c_id, B) < live_frames)
        pair_bias = jnp.where(pair_on, 0.0, -jnp.inf).astype(jnp.float32)
        t_id = lax.broadcasted_iota(jnp.int32, (T, 1), 0)
        t_pos = lax.rem(t_id, B)
        t_on = lax.div(t_id, B) < live_frames

        def temporal(p0):
            x = spat[:, pl.ds(p0, B), :].reshape(T, D)
            inv = lax.rsqrt(jnp.sum(x * x, axis=-1, keepdims=True) * (1.0 / D) + 1e-6)
            xb = x.astype(jnp.bfloat16)
            y = x * inv * gain
            hi = y.astype(jnp.bfloat16)
            lo = (y - hi.astype(jnp.float32)).astype(jnp.bfloat16)
            scores = lax.dot_general(
                jnp.concatenate([xb, xb], axis=1), jnp.concatenate([hi, lo], axis=1),
                (((1,), (1,)), ((), ())), preferred_element_type=jnp.float32,
            )
            scores = scores * inv + pair_bias
            top = jnp.max(scores, axis=-1, keepdims=True)
            weights = jnp.exp2(scores - top)
            total = jnp.sum(weights, axis=-1, keepdims=True)
            mixed = jnp.dot(weights.astype(jnp.bfloat16), xb, preferred_element_type=jnp.float32)
            live = jnp.where(t_on & (t_pos + p0 < live_pos), 1.0, 0.0).astype(jnp.float32)
            mixed = ((mixed / total) * live).astype(jnp.bfloat16).astype(jnp.float32)
            return (x + mixed).reshape(FRAMES, B, D)

        column = pl.ds(pl.multiple_of(my_head * D, D), D)
        for pc in range(PCHUNKS):

            def blocks(b, _):
                p0 = pl.multiple_of(pc * PC + b * 16, 16)
                pair = jnp.concatenate([temporal(p0), temporal(p0 + 8)], axis=1)
                sendbuf[:, pl.ds(p0, 16), :] = pair.astype(jnp.bfloat16)
                return 0

            lax.fori_loop(0, PC // 16, blocks, 0)
            span = pl.ds(pc * PC, PC)

            def send_frame(i, _):
                f = lax.rem(my_s + i, 16)
                pltpu.make_async_remote_copy(
                    sendbuf.at[f, span], out.at[0, 0, span, column], out_send, out_recv,
                    device_id=(my_g, f), device_id_type=MESH,
                ).start()
                return 0

            lax.fori_loop(1, 16, send_frame, 0)
            pltpu.make_async_copy(sendbuf.at[my_s, span], out.at[0, 0, span, column], out_recv).start()

        sent = recv.at[:, :, pl.ds(0, 95)]
        pltpu.make_async_copy(sent, sent, in_send).wait()
        mine = sendbuf.at[pl.ds(0, 15)]
        pltpu.make_async_copy(mine, mine, out_send).wait()

    @pl.when(jnp.logical_not(active))
    def _():
        sent = recv.at[:, :, pl.ds(0, 96)]
        pltpu.make_async_copy(sent, sent, in_send).wait()

    pltpu.make_async_copy(out, out, out_recv).wait()


def on_device(
    queries, key_rows, values, query_gain, key_gain, frames_per_clip, latent_height, latent_width, clip_plan
):
    def by_head(x):
        return x.reshape(16, FRAMES, 2, HEADS, D).transpose(0, 1, 3, 2, 4)

    smem = pl.BlockSpec(memory_space=pltpu.SMEM)
    hbm = pl.BlockSpec(memory_space=pl.ANY)
    vmem = pl.BlockSpec(memory_space=pltpu.VMEM)
    return pl.pallas_call(
        kernel,
        out_shape=jax.ShapeDtypeStruct((1, 1, POS, HEADS * D), jnp.bfloat16),
        in_specs=[smem] * 4 + [hbm] * 3 + [vmem] * 2,
        out_specs=hbm,
        scratch_shapes=[
            pltpu.VMEM((16, FRAMES, HEADS, 2, D), jnp.bfloat16),
            pltpu.VMEM((16, FRAMES, HEADS, 2, D), jnp.bfloat16),
            pltpu.VMEM((16, FRAMES, HEADS, 2, D), jnp.bfloat16),
            pltpu.VMEM((8, 3, FRAMES, HEADS, 2, D), jnp.bfloat16),
            pltpu.VMEM((3, FRAMES, DEVS, 2, D), jnp.bfloat16),
            pltpu.VMEM((FRAMES, POS, D), jnp.float32),
            pltpu.VMEM((FRAMES, POS, D), jnp.bfloat16),
            pltpu.SemaphoreType.DMA((3,)),
            pltpu.SemaphoreType.DMA,
            pltpu.SemaphoreType.DMA((CHUNKS,)),
            pltpu.SemaphoreType.DMA,
            pltpu.SemaphoreType.DMA,
            pltpu.SemaphoreType.REGULAR,
        ],
        compiler_params=pltpu.CompilerParams(
            collective_id=0, has_side_effects=True, vmem_limit_bytes=48 << 20
        ),
        name="attend",
    )(
        clip_plan, frames_per_clip, latent_height, latent_width,
        by_head(queries), by_head(key_rows), by_head(values),
        query_gain.reshape(1, D), key_gain.reshape(1, D),
    )


def solution(mesh):
    split = P(None, None, ("grp", "sp"), None)
    return jax.shard_map(
        on_device,
        mesh=mesh,
        in_specs=(split, split, split, P(), P(), P(), P(), P(), P()),
        out_specs=P("grp", "sp", None, None),
        check_vma=False,
    )
```

```python
import functools
import math

import jax
import jax.numpy as jnp
from jax import lax
from jax.experimental import pallas as pl
from jax.experimental.pallas import tpu as pltpu
from jax.sharding import PartitionSpec as P

MESH = pl.DeviceIdType.MESH
D = 128
HEADS = 12
FRAMES = 16
POS = 256
DEVS = 128
HALF = FRAMES // 2
BLOCK = 16
PC = 64
VMEM_BYTES = 64 << 20
SU = 4
SCALE2 = D**-0.5 * math.log2(math.e)


def unit_of(z, c, x, y):
    whole = x * 4 + y
    over = jnp.where(whole >= HEADS, 1, 0)
    group = jnp.where(c == 0, 2 * z + over, 2 * z + 1)
    head = jnp.where(c == 0, whole - HEADS * over, 4 + 2 * x + lax.div(y, 2))
    first_frame = jnp.where(c == 0, 0, HALF * lax.rem(y, 2))
    return group, head, first_frame


def kernel(
    plan_hbm, frames_hbm, height_hbm, width_hbm, q_hbm, k_hbm, v_hbm, gq_hbm, gk_hbm, out,
    plan, frames, height, width, gq, gk, xq, xk, xv, stage, recv, spat, sendbuf,
    x_sem, in_send, in_recv, pair_send, pair_recv, out_send, out_recv, ready,
):
    my_g = lax.axis_index("grp")
    my_s = lax.axis_index("sp")
    me = my_g * 16 + my_s
    mz, mc = lax.div(my_g, 2), lax.rem(my_g, 2)
    mx, my = lax.div(my_s, 4), lax.rem(my_s, 4)
    my_unit, my_head, my_first = unit_of(mz, mc, mx, my)

    barrier = pltpu.get_barrier_semaphore()

    def greet_grp(i, _):
        pl.semaphore_signal(barrier, 1, device_id=(lax.rem(my_g + i, 8), my_s), device_id_type=MESH)
        return 0

    def greet_sp(i, _):
        pl.semaphore_signal(barrier, 1, device_id=(my_g, lax.rem(my_s + i, 16)), device_id_type=MESH)
        return 0

    def greet_all(i, _):
        pl.semaphore_signal(ready, 1, device_id=(my_g, lax.rem(my_s + i, 16)), device_id_type=MESH)
        return 0

    lax.fori_loop(1, 8, greet_grp, 0)
    lax.fori_loop(1, 16, greet_sp, 0)
    loads = [
        pltpu.make_async_copy(ref, held, x_sem.at[t])
        for t, (ref, held) in enumerate((
            (plan_hbm, plan), (q_hbm, xq), (k_hbm, xk), (v_hbm, xv), (frames_hbm, frames),
            (height_hbm, height), (width_hbm, width), (gq_hbm, gq), (gk_hbm, gk),
        ))
    ]
    for copy in loads:
        copy.start()
    pl.semaphore_wait(barrier, 22)
    lax.fori_loop(1, 16, greet_all, 0)

    loads[0].wait()
    stage_rows = stage.reshape(8, 3, FRAMES * HEADS * 2, D)
    for t, held in enumerate((xq, xk, xv)):
        loads[1 + t].wait()
        x_rows = held.reshape(16, FRAMES * HEADS * 2, D)

        def pick(g, _):
            stage_rows[g, t] = x_rows[plan[g]]
            return 0

        lax.fori_loop(0, 8, pick, 0)
    for copy in loads[4:]:
        copy.wait()
    pl.semaphore_wait(ready, 15)

    def target(j, c):
        z = lax.rem(mz + lax.rem(j, 4), 4)
        x = lax.rem(mx + lax.rem(lax.div(j, 4), 4), 4)
        y = lax.rem(my + lax.div(j, 16), 4)
        return z, x, y

    def send_unit(part, j, c):
        z, x, y = target(j, c)
        group, head, first = unit_of(z, c, x, y)
        g, s = 2 * z + c, 4 * x + y
        src = stage.at[group, :, pl.ds(first + part * HALF, HALF), head]
        dst = recv.at[:, pl.ds(part * HALF, HALF), me]
        here = (j == 0) & (c == mc)

        @pl.when(jnp.logical_not(here))
        def _():
            pltpu.make_async_remote_copy(
                src, dst, in_send.at[part], in_recv.at[part], device_id=(g, s), device_id_type=MESH
            ).start()

        @pl.when(here)
        def _():
            pltpu.make_async_copy(src, dst, in_recv.at[part]).start()

    def send_first(i, _):
        j = lax.rem(i * 45, 128)
        send_unit(0, lax.div(j, 2), lax.rem(mc + lax.rem(j, 2), 2))
        return 0

    def send_second(i, _):
        send_unit(1, lax.rem(i * 29, 64), 0)
        return 0

    lax.fori_loop(0, 128, send_first, 0)
    lax.fori_loop(0, 64, send_second, 0)

    clip = plan[my_unit]
    live_frames = frames[clip]
    live_pos = height[clip] * width[clip]
    rows = recv.reshape(3, FRAMES, POS, D)
    key_bias = jnp.where(lax.broadcasted_iota(jnp.int32, (1, POS), 1) < live_pos, 0.0, -jnp.inf)
    row_live = jnp.where(lax.broadcasted_iota(jnp.int32, (POS, 1), 0) < live_pos, 1.0, 0.0)
    ones = jnp.ones((POS, D), jnp.bfloat16)

    def spatial(i):
        scores = lax.dot_general(
            rows[0, i], rows[1, i], (((1,), (1,)), ((), ())), preferred_element_type=jnp.float32
        )
        scores = scores + key_bias
        top = jnp.max(scores, axis=-1, keepdims=True)
        weights = jnp.exp2((scores - top) * SCALE2)
        total = jnp.sum(weights, axis=-1, keepdims=True)
        mixed = jnp.dot(weights.astype(jnp.bfloat16), rows[2, i], preferred_element_type=jnp.float32)
        f = my_first + i
        on = jnp.where(f < live_frames, 1.0, 0.0)
        spat[f] = (mixed * (row_live * on / total)).astype(jnp.bfloat16)

    def spatial_part(part):
        arrived = recv.at[:, pl.ds(part * HALF, HALF)]
        pltpu.make_async_copy(arrived, arrived, in_recv.at[part]).wait()

        def four(b, _):
            for k in range(SU):
                spatial(part * HALF + b * SU + k)
            return 0

        lax.fori_loop(0, HALF // SU, four, 0)

    spatial_part(0)

    @pl.when(mc == 0)
    def _():
        spatial_part(1)

    half = lax.rem(my, 2)
    own = pl.ds(pl.multiple_of(half * (POS // 2), POS // 2), POS // 2)
    theirs = pl.ds(pl.multiple_of((1 - half) * (POS // 2), POS // 2), POS // 2)

    @pl.when(mc == 1)
    def _():
        partner = my_s + 1 - 2 * half
        block = spat.at[pl.ds(my_first, HALF), theirs]
        copy = pltpu.make_async_remote_copy(
            block, block, pair_send, pair_recv, device_id=(my_g, partner), device_id_type=MESH
        )
        copy.start()
        copy.wait()

    gain = (gq[...] * gk[...]) * SCALE2
    T = FRAMES * BLOCK
    r_id = lax.broadcasted_iota(jnp.int32, (T, T), 0)
    c_id = lax.broadcasted_iota(jnp.int32, (T, T), 1)
    pair_on = (lax.rem(r_id, BLOCK) == lax.rem(c_id, BLOCK)) & (lax.div(c_id, BLOCK) < live_frames)
    pair_bias = jnp.where(pair_on, 0.0, -jnp.inf)
    t_on = lax.div(lax.broadcasted_iota(jnp.int32, (T, 1), 0), BLOCK) < live_frames
    frame_on = jnp.where(t_on, 1.0, 0.0)

    def temporal(p0):
        xb = spat[:, pl.ds(p0, BLOCK), :].reshape(T, D)
        x = xb.astype(jnp.float32)
        inv = lax.rsqrt(jnp.sum(x * x, axis=-1, keepdims=True) * (1.0 / D) + 1e-6)
        y = x * inv * gain
        hi = y.astype(jnp.bfloat16)
        lo = (y - hi.astype(jnp.float32)).astype(jnp.bfloat16)
        scores = lax.dot_general(
            jnp.concatenate([xb, xb], axis=1), jnp.concatenate([hi, lo], axis=1),
            (((1,), (1,)), ((), ())), preferred_element_type=jnp.float32,
        )
        scores = scores + pair_bias
        top = jnp.max(scores, axis=-1, keepdims=True)
        weights = jnp.exp2((scores - top) * inv)
        total = jnp.sum(weights, axis=-1, keepdims=True)
        mixed = jnp.dot(weights.astype(jnp.bfloat16), xb, preferred_element_type=jnp.float32)
        mixed = (mixed * (frame_on / total)).astype(jnp.bfloat16).astype(jnp.float32)
        sendbuf[:, pl.ds(p0, BLOCK), :] = (x + mixed).astype(jnp.bfloat16).reshape(FRAMES, BLOCK, D)

    column = pl.ds(pl.multiple_of(my_head * D, D), D)
    own_unit = my_unit == my_g

    def chunk(b, _):
        p0 = pl.multiple_of(b * PC, PC)
        for k in range(PC // BLOCK):
            temporal(p0 + k * BLOCK)
        span = pl.ds(p0, PC)

        def send_frame(i, _):
            f = lax.rem(my_s + i, 16)
            src, dst = sendbuf.at[f, span], out.at[0, 0, span, column]
            here = (i == 0) & own_unit

            @pl.when(jnp.logical_not(here))
            def _():
                pltpu.make_async_remote_copy(
                    src, dst, out_send, out_recv, device_id=(my_unit, f), device_id_type=MESH
                ).start()

            @pl.when(here)
            def _():
                pltpu.make_async_copy(src, dst, out_recv).start()

            return 0

        lax.fori_loop(0, 16, send_frame, 0)
        return 0

    first_chunk = jnp.where(mc == 0, 0, half * (POS // 2 // PC))
    last_chunk = jnp.where(mc == 0, POS // PC, first_chunk + POS // 2 // PC)
    lax.fori_loop(first_chunk, last_chunk, chunk, 0)

    def sent(ref, sem):
        pltpu.make_async_copy(ref, ref, sem).wait()

    sent(recv.at[:, pl.ds(0, HALF), pl.ds(0, DEVS - 1)], in_send.at[0])

    @pl.when(mc == 0)
    def _():
        sent(recv.at[:, pl.ds(0, HALF), pl.ds(0, DEVS // 2 - 1)], in_send.at[1])

        @pl.when(own_unit)
        def _():
            sent(sendbuf.at[pl.ds(0, 15)], out_send)

        @pl.when(jnp.logical_not(own_unit))
        def _():
            sent(sendbuf, out_send)

    @pl.when(mc == 1)
    def _():
        sent(recv.at[:, pl.ds(0, HALF), pl.ds(0, DEVS // 2)], in_send.at[1])
        sent(sendbuf.at[pl.ds(0, 15), pl.ds(0, POS // 2)], out_send)

    pltpu.make_async_copy(out, out, out_recv).wait()


def on_device(
    queries, key_rows, values, query_gain, key_gain, frames_per_clip, latent_height, latent_width, clip_plan
):
    def by_head(x):
        return x.reshape(16, FRAMES, 2, HEADS, D).transpose(0, 1, 3, 2, 4)

    hbm = pl.BlockSpec(memory_space=pl.ANY)
    clips = pltpu.VMEM((16, FRAMES, HEADS, 2, D), jnp.bfloat16)
    counts = pltpu.SMEM((16,), jnp.int32)
    dma = pltpu.SemaphoreType.DMA
    return pl.pallas_call(
        kernel,
        out_shape=jax.ShapeDtypeStruct((1, 1, POS, HEADS * D), jnp.bfloat16),
        in_specs=[hbm] * 9,
        out_specs=hbm,
        scratch_shapes=[
            pltpu.SMEM((8,), jnp.int32), counts, counts, counts,
            pltpu.VMEM((1, D), jnp.float32), pltpu.VMEM((1, D), jnp.float32),
            clips, clips, clips,
            pltpu.VMEM((8, 3, FRAMES, HEADS, 2, D), jnp.bfloat16),
            pltpu.VMEM((3, FRAMES, DEVS, 2, D), jnp.bfloat16),
            pltpu.VMEM((FRAMES, POS, D), jnp.bfloat16),
            pltpu.VMEM((FRAMES, POS, D), jnp.bfloat16),
            dma((9,)), dma((2,)), dma((2,)), dma, dma, dma, dma,
            pltpu.SemaphoreType.REGULAR,
        ],
        compiler_params=pltpu.CompilerParams(
            collective_id=0, has_side_effects=True, vmem_limit_bytes=VMEM_BYTES
        ),
        name="attend",
    )(
        clip_plan, frames_per_clip, latent_height, latent_width,
        by_head(queries), by_head(key_rows), by_head(values),
        query_gain.reshape(1, D), key_gain.reshape(1, D),
    )


def solution(mesh):
    split = P(None, None, ("grp", "sp"), None)
    return jax.shard_map(
        on_device,
        mesh=mesh,
        in_specs=(split, split, split, P(), P(), P(), P(), P(), P()),
        out_specs=P("grp", "sp", None, None),
        check_vma=False,
    )
```

```python
import functools
import math

import jax
import jax.numpy as jnp
from jax import lax
from jax.experimental import pallas as pl
from jax.experimental.pallas import tpu as pltpu
from jax.sharding import PartitionSpec as P

MESH = pl.DeviceIdType.MESH
D = 128
HEADS = 12
FRAMES = 16
POS = 256
DEVS = 128
HALF = FRAMES // 2
BLOCK = 16
PC = 128
VMEM_BYTES = 56 << 20
SU = 8
SCALE2 = D**-0.5 * math.log2(math.e)


def unit_of(z, c, x, y):
    whole = x * 4 + y
    over = jnp.where(whole >= HEADS, 1, 0)
    group = jnp.where(c == 0, 2 * z + over, 2 * z + 1)
    head = jnp.where(c == 0, whole - HEADS * over, 4 + 2 * x + lax.div(y, 2))
    first_frame = jnp.where(c == 0, 0, HALF * lax.rem(y, 2))
    return group, head, first_frame


def kernel(
    plan_hbm, frames_hbm, height_hbm, width_hbm, q_hbm, k_hbm, v_hbm, gq_hbm, gk_hbm, out,
    plan, frames, height, width, gq, gk, xq, xk, xv, stage, recv, spat, sendbuf, pair_bias,
    x_sem, in_send, in_recv, pair_send, pair_recv, out_send, out_recv, ready, mate,
):
    my_g = lax.axis_index("grp")
    my_s = lax.axis_index("sp")
    me = my_g * 16 + my_s
    mz, mc = lax.div(my_g, 2), lax.rem(my_g, 2)
    mx, my = lax.div(my_s, 4), lax.rem(my_s, 4)
    my_unit, my_head, my_first = unit_of(mz, mc, mx, my)

    barrier = pltpu.get_barrier_semaphore()
    loads = [
        pltpu.make_async_copy(ref, held, x_sem.at[t])
        for t, (ref, held) in enumerate((
            (plan_hbm, plan), (q_hbm, xq), (k_hbm, xk), (v_hbm, xv), (frames_hbm, frames),
            (height_hbm, height), (width_hbm, width), (gq_hbm, gq), (gk_hbm, gk),
        ))
    ]

    def greet_grp(i, _):
        pl.semaphore_signal(barrier, 1, device_id=(lax.rem(my_g + i, 8), my_s), device_id_type=MESH)
        return 0

    def greet_sp(i, _):
        pl.semaphore_signal(barrier, 1, device_id=(my_g, lax.rem(my_s + i, 16)), device_id_type=MESH)
        return 0

    def greet_all(i, _):
        pl.semaphore_signal(ready, 1, device_id=(lax.rem(my_g + i, 8), my_s), device_id_type=MESH)
        return 0

    for copy in loads[:4]:
        copy.start()
    lax.fori_loop(1, 16, greet_sp, 0)
    lax.fori_loop(1, 8, greet_grp, 0)
    for copy in loads[4:]:
        copy.start()

    def wait_bytes(ref, sem):
        pltpu.make_async_copy(ref, ref, sem).wait()

    def sent(part, to_core):
        def of(count):
            wait_bytes(recv.at[:, pl.ds(0, HALF), pl.ds(0, count)], in_send.at[part])

        @pl.when(mc == to_core)
        def _():
            of(DEVS // 2 - 1)

        @pl.when(mc != to_core)
        def _():
            of(DEVS // 2)

    stage_rows = stage.reshape(8, 3, FRAMES * HEADS * 2, D)

    def pick(t, held, z):
        x_rows = held.reshape(16, FRAMES * HEADS * 2, D)
        for c in range(2):
            stage_rows[2 * z + c, t] = x_rows[plan[2 * z + c]]

    def send(src, dst, sem, arrival, z, c, x, y):
        here = (z == mz) & (c == mc) & (x == mx) & (y == my)

        @pl.when(jnp.logical_not(here))
        def _():
            pltpu.make_async_remote_copy(
                src, dst, in_send.at[sem], in_recv.at[arrival],
                device_id=(2 * z + c, 4 * x + y), device_id_type=MESH,
            ).start()

        @pl.when(here)
        def _():
            pltpu.make_async_copy(src, dst, in_recv.at[arrival]).start()

    def send_half(z, x, y):
        group, head, first = unit_of(z, 1, x, y)
        send(
            stage.at[group, :, pl.ds(first, HALF), head], recv.at[:, pl.ds(0, HALF), me], 0, 0, z, 1, x, y
        )

    def send_part(part, z, x, y):
        group, head, _ = unit_of(z, 0, x, y)
        span = pl.ds(part * HALF, HALF)
        send(stage.at[group, :, span, head], recv.at[:, span, me], 1 + part, part, z, 0, x, y)

    def near(i):
        return mz, lax.rem(mx + lax.div(i, 4), 4), lax.rem(my + lax.rem(i, 4), 4)

    def plane(c):
        @pl.when(c == 1)
        def _():
            def body(i, _):
                send_half(*near(lax.rem(i * 5, 16)))
                return 0

            lax.fori_loop(0, 16, body, 0)

        @pl.when(c == 0)
        def _():
            def body(i, _):
                pass
                return 0

            lax.fori_loop(0, 16, body, 0)

    def column(i, _):
        z = lax.rem(mz + i, 4)
        send_half(z, mx, my)
        return 0

    def far(i, start):
        j = lax.rem(i * 7 + 22 * mc + start, 45)
        d = 1 + lax.div(j, 3)
        return lax.rem(mz + 1 + lax.rem(j, 3), 4), lax.rem(mx + lax.div(d, 4), 4), lax.rem(my + lax.rem(d, 4), 4)

    pl.semaphore_wait(barrier, 22)
    pl.semaphore_signal(mate, 1, device_id=(my_g + 1 - 2 * mc, my_s), device_id_type=MESH)
    lax.fori_loop(1, 8, greet_all, 0)
    loads[0].wait()
    for t, held in enumerate((xq, xk, xv)):
        loads[1 + t].wait()
        pick(t, held, mz)
    plane(mc)
    pl.semaphore_wait(mate, 1)
    plane(1 - mc)

    def pick_others(i, _):
        for t, held in enumerate((xq, xk, xv)):
            pick(t, held, lax.rem(mz + i, 4))
        return 0

    lax.fori_loop(1, 4, pick_others, 0)
    lax.fori_loop(1, 4, column, 0)
    pl.semaphore_wait(ready, 7)

    def far_half(i, _):
        send_half(*far(i, 0))
        return 0

    def first(i, _):
        send_part(0, *anywhere(i))
        return 0

    def second(i, _):
        send_part(1, *anywhere(i))
        return 0

    def anywhere(i):
        j = lax.rem(i * 29 + 32 * mc, 64)
        return lax.rem(mz + lax.rem(j, 4), 4), lax.rem(mx + lax.rem(lax.div(j, 4), 4), 4), lax.rem(my + lax.div(j, 16), 4)

    lax.fori_loop(0, 45, far_half, 0)
    lax.fori_loop(0, 64, first, 0)
    lax.fori_loop(0, 64, second, 0)
    for copy in loads[4:]:
        copy.wait()

    clip = plan[my_unit]
    live_frames = frames[clip]
    live_pos = height[clip] * width[clip]
    rows = recv.reshape(3, FRAMES, POS, D)
    key_bias = jnp.where(lax.broadcasted_iota(jnp.int32, (1, POS), 1) < live_pos, 0.0, -jnp.inf)

    def attend(q, i, live):
        scores = lax.dot_general(q, rows[1, i], (((1,), (1,)), ((), ())), preferred_element_type=jnp.float32)
        scores = scores + key_bias
        top = jnp.max(scores, axis=-1, keepdims=True)
        weights = jnp.exp2((scores - top) * SCALE2)
        total = jnp.sum(weights, axis=-1, keepdims=True)
        mixed = jnp.dot(weights.astype(jnp.bfloat16), rows[2, i], preferred_element_type=jnp.float32)
        on = jnp.where(my_first + i < live_frames, 1.0, 0.0)
        return (mixed * (live * on / total)).astype(jnp.bfloat16)

    gain = (gq[...] * gk[...]) * SCALE2
    T = FRAMES * BLOCK
    r_id = lax.broadcasted_iota(jnp.int32, (T, T), 0)
    c_id = lax.broadcasted_iota(jnp.int32, (T, T), 1)
    pair_on = (lax.rem(r_id, BLOCK) == lax.rem(c_id, BLOCK)) & (lax.div(c_id, BLOCK) < live_frames)
    pair_bias[...] = jnp.where(pair_on, 0.0, -jnp.inf)
    t_on = lax.div(lax.broadcasted_iota(jnp.int32, (T, 1), 0), BLOCK) < live_frames
    frame_on = jnp.where(t_on, 1.0, 0.0)

    def temporal(p0):
        xb = spat[:, pl.ds(p0, BLOCK), :].reshape(T, D)
        x = xb.astype(jnp.float32)
        inv = lax.rsqrt(jnp.sum(x * x, axis=-1, keepdims=True) * (1.0 / D) + 1e-6)
        y = x * inv * gain
        hi = y.astype(jnp.bfloat16)
        lo = (y - hi.astype(jnp.float32)).astype(jnp.bfloat16)
        scores = lax.dot_general(
            jnp.concatenate([xb, xb], axis=1), jnp.concatenate([hi, lo], axis=1),
            (((1,), (1,)), ((), ())), preferred_element_type=jnp.float32,
        )
        scores = scores + pair_bias[...]
        top = jnp.max(scores, axis=-1, keepdims=True)
        weights = jnp.exp2((scores - top) * inv)
        total = jnp.sum(weights, axis=-1, keepdims=True)
        mixed = jnp.dot(weights.astype(jnp.bfloat16), xb, preferred_element_type=jnp.float32)
        mixed = (mixed * (frame_on / total)).astype(jnp.bfloat16).astype(jnp.float32)
        sendbuf[:, pl.ds(p0, BLOCK), :] = (x + mixed).astype(jnp.bfloat16).reshape(FRAMES, BLOCK, D)

    head_lanes = pl.ds(pl.multiple_of(my_head * D, D), D)
    own_unit = my_unit == my_g

    def chunk(p0):
        for k in range(PC // BLOCK):
            temporal(p0 + k * BLOCK)
        span = pl.ds(p0, PC)

        def send_frame(i, _):
            f = lax.rem(my_s + i, 16)
            src, dst = sendbuf.at[f, span], out.at[0, 0, span, head_lanes]
            here = (i == 0) & own_unit

            @pl.when(jnp.logical_not(here))
            def _():
                pltpu.make_async_remote_copy(
                    src, dst, out_send, out_recv, device_id=(my_unit, f), device_id_type=MESH
                ).start()

            @pl.when(here)
            def _():
                pltpu.make_async_copy(src, dst, out_recv).start()

            return 0

        lax.fori_loop(0, 16, send_frame, 0)

    @pl.when(mc == 1)
    def _():
        wait_bytes(recv.at[:, pl.ds(0, HALF)], in_recv.at[0])
        live = jnp.where(lax.broadcasted_iota(jnp.int32, (POS, 1), 0) < live_pos, 1.0, 0.0)

        def group(b, _):
            for k in range(SU):
                i = b * SU + k
                spat[my_first + i] = attend(rows[0, i], i, live)
            return 0

        lax.fori_loop(0, HALF // SU, group, 0)

        half = lax.rem(my, 2)
        theirs = pl.ds(pl.multiple_of((1 - half) * (POS // 2), POS // 2), POS // 2)
        block = spat.at[pl.ds(my_first, HALF), theirs]
        copy = pltpu.make_async_remote_copy(
            block, block, pair_send, pair_recv, device_id=(my_g, my_s + 1 - 2 * half), device_id_type=MESH
        )
        copy.start()
        copy.wait()

        def half_chunk(k, _):
            chunk(pl.multiple_of(half * (POS // 2) + k * PC, PC))
            return 0

        lax.fori_loop(0, POS // 2 // PC, half_chunk, 0)
        wait_bytes(sendbuf.at[pl.ds(0, 15), pl.ds(0, POS // 2)], out_send)

    @pl.when(mc == 0)
    def _():
        live = jnp.where(lax.broadcasted_iota(jnp.int32, (POS, 1), 0) < live_pos, 1.0, 0.0)

        def part(k, _):
            wait_bytes(recv.at[:, pl.ds(0, HALF)], in_recv.at[k])

            def group(b, _):
                for u in range(SU):
                    i = k * HALF + b * SU + u
                    spat[i] = attend(rows[0, i], i, live)
                return 0

            lax.fori_loop(0, HALF // SU, group, 0)
            return 0

        lax.fori_loop(0, 2, part, 0)

        def all_chunks(k, _):
            chunk(pl.multiple_of(k * PC, PC))
            return 0

        lax.fori_loop(0, POS // PC, all_chunks, 0)

        @pl.when(own_unit)
        def _():
            wait_bytes(sendbuf.at[pl.ds(0, 15)], out_send)

        @pl.when(jnp.logical_not(own_unit))
        def _():
            wait_bytes(sendbuf, out_send)

    sent(0, 1)
    sent(1, 0)
    sent(2, 0)
    wait_bytes(out, out_recv)


def on_device(
    queries, key_rows, values, query_gain, key_gain, frames_per_clip, latent_height, latent_width, clip_plan
):
    def by_head(x):
        return x.reshape(16, FRAMES, 2, HEADS, D).transpose(0, 1, 3, 2, 4)

    hbm = pl.BlockSpec(memory_space=pl.ANY)
    clips = pltpu.VMEM((16, FRAMES, HEADS, 2, D), jnp.bfloat16)
    counts = pltpu.SMEM((16,), jnp.int32)
    dma = pltpu.SemaphoreType.DMA
    return pl.pallas_call(
        kernel,
        out_shape=pltpu.VMEM((1, 1, POS, HEADS * D), jnp.bfloat16),
        in_specs=[hbm] * 9,
        out_specs=hbm,
        scratch_shapes=[
            pltpu.SMEM((8,), jnp.int32), counts, counts, counts,
            pltpu.VMEM((1, D), jnp.float32), pltpu.VMEM((1, D), jnp.float32),
            clips, clips, clips,
            pltpu.VMEM((8, 3, FRAMES, HEADS, 2, D), jnp.bfloat16),
            pltpu.VMEM((3, FRAMES, DEVS, 2, D), jnp.bfloat16),
            pltpu.VMEM((FRAMES, POS, D), jnp.bfloat16),
            pltpu.VMEM((FRAMES, POS, D), jnp.bfloat16),
            pltpu.VMEM((FRAMES * BLOCK, FRAMES * BLOCK), jnp.float32),
            dma((9,)), dma((3,)), dma((2,)), dma, dma, dma, dma,
            pltpu.SemaphoreType.REGULAR, pltpu.SemaphoreType.REGULAR,
        ],
        compiler_params=pltpu.CompilerParams(
            collective_id=0, has_side_effects=True, vmem_limit_bytes=VMEM_BYTES
        ),
        name="attend",
    )(
        clip_plan, frames_per_clip, latent_height, latent_width,
        by_head(queries), by_head(key_rows), by_head(values),
        query_gain.reshape(1, D), key_gain.reshape(1, D),
    )


def solution(mesh):
    split = P(None, None, ("grp", "sp"), None)
    return jax.shard_map(
        on_device,
        mesh=mesh,
        in_specs=(split, split, split, P(), P(), P(), P(), P(), P()),
        out_specs=P("grp", "sp", None, None),
        check_vma=False,
    )
```

```python
import functools
import math

import jax
import jax.numpy as jnp
from jax import lax
from jax.experimental import pallas as pl
from jax.experimental.pallas import tpu as pltpu
from jax.sharding import PartitionSpec as P

MESH = pl.DeviceIdType.MESH
D = 128
HEADS = 12
FRAMES = 16
POS = 256
DEVS = 128
HALF = FRAMES // 2
BLOCK = 16
PC = 128
VMEM_BYTES = 56 << 20
SU = 8
LU = 8
TU = 8
SCALE2 = D**-0.5 * math.log2(math.e)


def unit_of(z, c, x, y):
    whole = x * 4 + y
    over = jnp.where(whole >= HEADS, 1, 0)
    group = jnp.where(c == 0, 2 * z + over, 2 * z + 1)
    head = jnp.where(c == 0, whole - HEADS * over, 4 + 2 * x + lax.div(y, 2))
    first_frame = jnp.where(c == 0, 0, HALF * lax.rem(y, 2))
    return group, head, first_frame


def kernel(
    plan_hbm, frames_hbm, height_hbm, width_hbm, q_hbm, k_hbm, v_hbm, gq_hbm, gk_hbm, out,
    plan, frames, height, width, gq, gk, xq, xk, xv, stage, recv, spat, sendbuf, pair_bias,
    x_sem, in_send, in_recv, pair_send, pair_recv, out_send, out_recv, ready, mate,
):
    my_g = lax.axis_index("grp")
    my_s = lax.axis_index("sp")
    me = my_g * 16 + my_s
    mz, mc = lax.div(my_g, 2), lax.rem(my_g, 2)
    mx, my = lax.div(my_s, 4), lax.rem(my_s, 4)
    my_unit, my_head, my_first = unit_of(mz, mc, mx, my)

    barrier = pltpu.get_barrier_semaphore()
    loads = [
        pltpu.make_async_copy(ref, held, x_sem.at[t])
        for t, (ref, held) in enumerate((
            (plan_hbm, plan), (q_hbm, xq), (k_hbm, xk), (v_hbm, xv), (frames_hbm, frames),
            (height_hbm, height), (width_hbm, width), (gq_hbm, gq), (gk_hbm, gk),
        ))
    ]

    def greet_grp(i, _):
        pl.semaphore_signal(barrier, 1, device_id=(lax.rem(my_g + i, 8), my_s), device_id_type=MESH)
        return 0

    def greet_sp(i, _):
        pl.semaphore_signal(barrier, 1, device_id=(my_g, lax.rem(my_s + i, 16)), device_id_type=MESH)
        return 0

    def greet_all(i, _):
        pl.semaphore_signal(ready, 1, device_id=(lax.rem(my_g + i, 8), my_s), device_id_type=MESH)
        return 0

    for copy in loads[:4]:
        copy.start()
    lax.fori_loop(1, 16, greet_sp, 0)
    lax.fori_loop(1, 8, greet_grp, 0)
    for copy in loads[4:]:
        copy.start()

    def wait_bytes(ref, sem):
        pltpu.make_async_copy(ref, ref, sem).wait()

    def sent(part, to_core):
        def of(count):
            wait_bytes(recv.at[:, pl.ds(0, HALF), pl.ds(0, count)], in_send.at[part])

        @pl.when(mc == to_core)
        def _():
            of(DEVS // 2 - 1)

        @pl.when(mc != to_core)
        def _():
            of(DEVS // 2)

    stage_rows = stage.reshape(8, 3, FRAMES * HEADS * 2, D)

    def pick(t, held, z):
        x_rows = held.reshape(16, FRAMES * HEADS * 2, D)
        for c in range(2):
            stage_rows[2 * z + c, t] = x_rows[plan[2 * z + c]]

    def send(src, dst, sem, arrival, z, c, x, y):
        here = (z == mz) & (c == mc) & (x == mx) & (y == my)

        @pl.when(jnp.logical_not(here))
        def _():
            pltpu.make_async_remote_copy(
                src, dst, in_send.at[sem], in_recv.at[arrival],
                device_id=(2 * z + c, 4 * x + y), device_id_type=MESH,
            ).start()

        @pl.when(here)
        def _():
            pltpu.make_async_copy(src, dst, in_recv.at[arrival]).start()

    def send_half(z, x, y):
        group, head, first = unit_of(z, 1, x, y)
        send(
            stage.at[group, :, pl.ds(first, HALF), head], recv.at[:, pl.ds(0, HALF), me], 0, 0, z, 1, x, y
        )

    def send_part(part, z, x, y):
        group, head, _ = unit_of(z, 0, x, y)
        span = pl.ds(part * HALF, HALF)
        send(stage.at[group, :, span, head], recv.at[:, span, me], 1 + part, part, z, 0, x, y)

    def near(i):
        return mz, lax.rem(mx + lax.div(i, 4), 4), lax.rem(my + lax.rem(i, 4), 4)

    def plane(c):
        @pl.when(c == 1)
        def _():
            def body(i, _):
                send_half(*near(lax.rem(i * 5, 16)))
                return 0

            lax.fori_loop(0, 16, body, 0)

        @pl.when(c == 0)
        def _():
            def body(i, _):
                pass
                return 0

            lax.fori_loop(0, 16, body, 0)

    def column(i, _):
        z = lax.rem(mz + i, 4)
        send_half(z, mx, my)
        return 0

    pl.semaphore_wait(barrier, 22)
    pl.semaphore_signal(mate, 1, device_id=(my_g + 1 - 2 * mc, my_s), device_id_type=MESH)
    lax.fori_loop(1, 8, greet_all, 0)
    loads[0].wait()
    for t, held in enumerate((xq, xk, xv)):
        loads[1 + t].wait()
        pick(t, held, mz)
    plane(mc)
    pl.semaphore_wait(mate, 1)
    plane(1 - mc)

    def pick_others(i, _):
        for t, held in enumerate((xq, xk, xv)):
            pick(t, held, lax.rem(mz + i, 4))
        return 0

    lax.fori_loop(1, 4, pick_others, 0)
    lax.fori_loop(1, 4, column, 0)
    pl.semaphore_wait(ready, 7)

    def far_half(i, _):
        z, x, y = anywhere(i)

        @pl.when((z != mz) & ((x != mx) | (y != my)))
        def _():
            send_half(z, x, y)

        return 0

    def first(i, _):
        send_part(0, *anywhere(i))
        return 0

    def second(i, _):
        send_part(1, *anywhere(i))
        return 0

    def anywhere(i):
        j = lax.rem(i * 29 + 32 * mc, 64)
        return lax.rem(mz + lax.rem(j, 4), 4), lax.rem(mx + lax.rem(lax.div(j, 4), 4), 4), lax.rem(my + lax.div(j, 16), 4)

    lax.fori_loop(0, 64, far_half, 0)
    lax.fori_loop(0, 64, first, 0)
    lax.fori_loop(0, 64, second, 0)
    for copy in loads[4:]:
        copy.wait()

    clip = plan[my_unit]
    live_frames = frames[clip]
    live_pos = height[clip] * width[clip]
    rows = recv.reshape(3, FRAMES, POS, D)
    key_bias = jnp.where(lax.broadcasted_iota(jnp.int32, (1, POS), 1) < live_pos, 0.0, -jnp.inf)

    def attend(q, i, live):
        scores = lax.dot_general(q, rows[1, i], (((1,), (1,)), ((), ())), preferred_element_type=jnp.float32)
        scores = scores + key_bias
        top = jnp.max(scores, axis=-1, keepdims=True)
        weights = jnp.exp2((scores - top) * SCALE2)
        total = jnp.sum(weights, axis=-1, keepdims=True)
        mixed = jnp.dot(weights.astype(jnp.bfloat16), rows[2, i], preferred_element_type=jnp.float32)
        on = jnp.where(my_first + i < live_frames, 1.0, 0.0)
        return (mixed * (live * on / total)).astype(jnp.bfloat16)

    gain = (gq[...] * gk[...]) * SCALE2
    T = FRAMES * BLOCK
    r_id = lax.broadcasted_iota(jnp.int32, (T, T), 0)
    c_id = lax.broadcasted_iota(jnp.int32, (T, T), 1)
    pair_on = (lax.rem(r_id, BLOCK) == lax.rem(c_id, BLOCK)) & (lax.div(c_id, BLOCK) < live_frames)
    pair_bias[...] = jnp.where(pair_on, 0.0, -jnp.inf)
    t_on = lax.div(lax.broadcasted_iota(jnp.int32, (T, 1), 0), BLOCK) < live_frames
    frame_on = jnp.where(t_on, 1.0, 0.0)

    def temporal(p0):
        xb = spat[:, pl.ds(p0, BLOCK), :].reshape(T, D)
        x = xb.astype(jnp.float32)
        inv = lax.rsqrt(jnp.sum(x * x, axis=-1, keepdims=True) * (1.0 / D) + 1e-6)
        y = x * inv * gain
        hi = y.astype(jnp.bfloat16)
        lo = (y - hi.astype(jnp.float32)).astype(jnp.bfloat16)
        scores = lax.dot_general(
            jnp.concatenate([xb, xb], axis=1), jnp.concatenate([hi, lo], axis=1),
            (((1,), (1,)), ((), ())), preferred_element_type=jnp.float32,
        )
        scores = scores + pair_bias[...]
        top = jnp.max(scores, axis=-1, keepdims=True)
        weights = jnp.exp2((scores - top) * inv)
        total = jnp.sum(weights, axis=-1, keepdims=True)
        mixed = jnp.dot(weights.astype(jnp.bfloat16), xb, preferred_element_type=jnp.float32)
        mixed = (mixed * (frame_on / total)).astype(jnp.bfloat16).astype(jnp.float32)
        sendbuf[:, pl.ds(p0, BLOCK), :] = (x + mixed).astype(jnp.bfloat16).reshape(FRAMES, BLOCK, D)

    head_lanes = pl.ds(pl.multiple_of(my_head * D, D), D)
    own_unit = my_unit == my_g

    def chunk(p0):
        def blocks(b, _):
            for k in range(TU):
                temporal(pl.multiple_of(p0 + (b * TU + k) * BLOCK, BLOCK))
            return 0

        lax.fori_loop(0, PC // BLOCK // TU, blocks, 0)
        span = pl.ds(p0, PC)

        def send_frame(i, _):
            f = lax.rem(my_s + i, 16)
            src, dst = sendbuf.at[f, span], out.at[0, 0, span, head_lanes]
            here = (i == 0) & own_unit

            @pl.when(jnp.logical_not(here))
            def _():
                pltpu.make_async_remote_copy(
                    src, dst, out_send, out_recv, device_id=(my_unit, f), device_id_type=MESH
                ).start()

            @pl.when(here)
            def _():
                pltpu.make_async_copy(src, dst, out_recv).start()

            return 0

        lax.fori_loop(0, 16, send_frame, 0)

    @pl.when(mc == 1)
    def _():
        wait_bytes(recv.at[:, pl.ds(0, HALF)], in_recv.at[0])
        live = jnp.where(lax.broadcasted_iota(jnp.int32, (POS, 1), 0) < live_pos, 1.0, 0.0)

        def group(b, _):
            for k in range(SU):
                i = b * SU + k
                spat[my_first + i] = attend(rows[0, i], i, live)
            return 0

        lax.fori_loop(0, HALF // SU, group, 0)

        half = lax.rem(my, 2)
        theirs = pl.ds(pl.multiple_of((1 - half) * (POS // 2), POS // 2), POS // 2)
        block = spat.at[pl.ds(my_first, HALF), theirs]
        copy = pltpu.make_async_remote_copy(
            block, block, pair_send, pair_recv, device_id=(my_g, my_s + 1 - 2 * half), device_id_type=MESH
        )
        copy.start()
        copy.wait()

        def half_chunk(k, _):
            chunk(pl.multiple_of(half * (POS // 2) + k * PC, PC))
            return 0

        lax.fori_loop(0, POS // 2 // PC, half_chunk, 0)
        wait_bytes(sendbuf.at[pl.ds(0, 15), pl.ds(0, POS // 2)], out_send)

    @pl.when(mc == 0)
    def _():
        live = jnp.where(lax.broadcasted_iota(jnp.int32, (POS, 1), 0) < live_pos, 1.0, 0.0)
        wait_bytes(recv.at[:, pl.ds(0, HALF)], in_recv.at[0])

        def first_frames(b, _):
            for k in range(SU):
                i = b * SU + k
                spat[i] = attend(rows[0, i], i, live)
            return 0

        lax.fori_loop(0, HALF // SU, first_frames, 0)

        wait_bytes(recv.at[:, pl.ds(0, HALF)], in_recv.at[1])

        def finish(c, _):
            p0 = pl.multiple_of(c * PC, PC)
            span = pl.ds(p0, PC)
            place = p0 + lax.broadcasted_iota(jnp.int32, (PC, 1), 0)
            on = jnp.where(place < live_pos, 1.0, 0.0)

            def last_frames(b, _):
                for k in range(LU):
                    i = HALF + b * LU + k
                    spat[i, span] = attend(rows[0, i, span], i, on)
                return 0

            lax.fori_loop(0, HALF // LU, last_frames, 0)
            chunk(p0)
            return 0

        lax.fori_loop(0, POS // PC, finish, 0)

        @pl.when(own_unit)
        def _():
            wait_bytes(sendbuf.at[pl.ds(0, 15)], out_send)

        @pl.when(jnp.logical_not(own_unit))
        def _():
            wait_bytes(sendbuf, out_send)

    sent(0, 1)
    sent(1, 0)
    sent(2, 0)
    wait_bytes(out, out_recv)


def on_device(
    queries, key_rows, values, query_gain, key_gain, frames_per_clip, latent_height, latent_width, clip_plan
):
    def by_head(x):
        return x.reshape(16, FRAMES, 2, HEADS, D).transpose(0, 1, 3, 2, 4)

    hbm = pl.BlockSpec(memory_space=pl.ANY)
    clips = pltpu.VMEM((16, FRAMES, HEADS, 2, D), jnp.bfloat16)
    counts = pltpu.SMEM((16,), jnp.int32)
    dma = pltpu.SemaphoreType.DMA
    return pl.pallas_call(
        kernel,
        out_shape=pltpu.VMEM((1, 1, POS, HEADS * D), jnp.bfloat16),
        in_specs=[hbm] * 9,
        out_specs=hbm,
        scratch_shapes=[
            pltpu.SMEM((8,), jnp.int32), counts, counts, counts,
            pltpu.VMEM((1, D), jnp.float32), pltpu.VMEM((1, D), jnp.float32),
            clips, clips, clips,
            pltpu.VMEM((8, 3, FRAMES, HEADS, 2, D), jnp.bfloat16),
            pltpu.VMEM((3, FRAMES, DEVS, 2, D), jnp.bfloat16),
            pltpu.VMEM((FRAMES, POS, D), jnp.bfloat16),
            pltpu.VMEM((FRAMES, POS, D), jnp.bfloat16),
            pltpu.VMEM((FRAMES * BLOCK, FRAMES * BLOCK), jnp.float32),
            dma((9,)), dma((3,)), dma((2,)), dma, dma, dma, dma,
            pltpu.SemaphoreType.REGULAR, pltpu.SemaphoreType.REGULAR,
        ],
        compiler_params=pltpu.CompilerParams(
            collective_id=0, has_side_effects=True, vmem_limit_bytes=VMEM_BYTES
        ),
        name="attend",
    )(
        clip_plan, frames_per_clip, latent_height, latent_width,
        by_head(queries), by_head(key_rows), by_head(values),
        query_gain.reshape(1, D), key_gain.reshape(1, D),
    )


def solution(mesh):
    split = P(None, None, ("grp", "sp"), None)
    return jax.shard_map(
        on_device,
        mesh=mesh,
        in_specs=(split, split, split, P(), P(), P(), P(), P(), P()),
        out_specs=P("grp", "sp", None, None),
        check_vma=False,
    )
```

```python
import functools
import math

import jax
import jax.numpy as jnp
from jax import lax
from jax.experimental import pallas as pl
from jax.experimental.pallas import tpu as pltpu
from jax.sharding import PartitionSpec as P

MESH = pl.DeviceIdType.MESH
D = 128
HEADS = 12
FRAMES = 16
POS = 256
DEVS = 128
HALF = FRAMES // 2
BLOCK = 16
PC = 128
VMEM_BYTES = 56 << 20
SU = 8
TIERS = ((0, 1, 3, 4, 12, 2, 8, 5), (7, 13, 15, 6, 9, 11, 14, 10))
LU = 8
TU = 8
SCALE2 = D**-0.5 * math.log2(math.e)


def unit_of(z, c, x, y):
    whole = x * 4 + y
    over = jnp.where(whole >= HEADS, 1, 0)
    group = jnp.where(c == 0, 2 * z + over, 2 * z + 1)
    head = jnp.where(c == 0, whole - HEADS * over, 4 + 2 * x + lax.div(y, 2))
    first_frame = jnp.where(c == 0, 0, HALF * lax.rem(y, 2))
    return group, head, first_frame


def kernel(
    plan_hbm, frames_hbm, height_hbm, width_hbm, q_hbm, k_hbm, v_hbm, gq_hbm, gk_hbm, out,
    plan, frames, height, width, gq, gk, xq, xk, xv, stage, recv, spat, sendbuf, pair_bias,
    x_sem, in_send, in_recv, pair_send, pair_recv, out_send, out_recv, ready, mate,
):
    my_g = lax.axis_index("grp")
    my_s = lax.axis_index("sp")
    me = my_g * 16 + my_s
    mz, mc = lax.div(my_g, 2), lax.rem(my_g, 2)
    mx, my = lax.div(my_s, 4), lax.rem(my_s, 4)
    my_unit, my_head, my_first = unit_of(mz, mc, mx, my)

    barrier = pltpu.get_barrier_semaphore()
    loads = [
        pltpu.make_async_copy(ref, held, x_sem.at[t])
        for t, (ref, held) in enumerate((
            (plan_hbm, plan), (q_hbm, xq), (k_hbm, xk), (v_hbm, xv), (frames_hbm, frames),
            (height_hbm, height), (width_hbm, width), (gq_hbm, gq), (gk_hbm, gk),
        ))
    ]

    def greet_grp(i, _):
        pl.semaphore_signal(barrier, 1, device_id=(lax.rem(my_g + i, 8), my_s), device_id_type=MESH)
        return 0

    def greet_sp(i, _):
        pl.semaphore_signal(barrier, 1, device_id=(my_g, lax.rem(my_s + i, 16)), device_id_type=MESH)
        return 0

    def greet_all(i, _):
        pl.semaphore_signal(ready, 1, device_id=(lax.rem(my_g + i, 8), my_s), device_id_type=MESH)
        return 0

    for copy in loads[:4]:
        copy.start()
    lax.fori_loop(1, 16, greet_sp, 0)
    lax.fori_loop(1, 8, greet_grp, 0)
    for copy in loads[4:]:
        copy.start()

    def wait_bytes(ref, sem):
        pltpu.make_async_copy(ref, ref, sem).wait()

    def sent(part, to_core):
        def of(count):
            wait_bytes(recv.at[:, pl.ds(0, HALF), pl.ds(0, count)], in_send.at[part])

        @pl.when(mc == to_core)
        def _():
            of(DEVS // 2 - 1)

        @pl.when(mc != to_core)
        def _():
            of(DEVS // 2)

    stage_rows = stage.reshape(8, 3, FRAMES * HEADS * 2, D)

    def pick(t, held, z):
        x_rows = held.reshape(16, FRAMES * HEADS * 2, D)
        for c in range(2):
            stage_rows[2 * z + c, t] = x_rows[plan[2 * z + c]]

    def send(src, dst, sem, arrival, z, c, x, y):
        here = (z == mz) & (c == mc) & (x == mx) & (y == my)

        @pl.when(jnp.logical_not(here))
        def _():
            pltpu.make_async_remote_copy(
                src, dst, in_send.at[sem], in_recv.at[arrival],
                device_id=(2 * z + c, 4 * x + y), device_id_type=MESH,
            ).start()

        @pl.when(here)
        def _():
            pltpu.make_async_copy(src, dst, in_recv.at[arrival]).start()

    def send_half(z, x, y):
        group, head, first = unit_of(z, 1, x, y)
        send(
            stage.at[group, :, pl.ds(first, HALF), head], recv.at[:, pl.ds(0, HALF), me], 0, 0, z, 1, x, y
        )

    def send_part(part, z, x, y):
        group, head, _ = unit_of(z, 0, x, y)
        span = pl.ds(part * HALF, HALF)
        send(stage.at[group, :, span, head], recv.at[:, span, me], 1 + part, part, z, 0, x, y)

    def near(i):
        return mz, lax.rem(mx + lax.div(i, 4), 4), lax.rem(my + lax.rem(i, 4), 4)

    def plane(c):
        @pl.when(c == 1)
        def _():
            def body(i, _):
                send_half(*near(lax.rem(i * 5, 16)))
                return 0

            lax.fori_loop(0, 16, body, 0)

        @pl.when(c == 0)
        def _():
            def body(i, _):
                pass
                return 0

            lax.fori_loop(0, 16, body, 0)

    def column(i, _):
        z = lax.rem(mz + i, 4)
        send_half(z, mx, my)
        return 0

    pl.semaphore_wait(barrier, 22)
    pl.semaphore_signal(mate, 1, device_id=(my_g + 1 - 2 * mc, my_s), device_id_type=MESH)
    lax.fori_loop(1, 8, greet_all, 0)
    loads[0].wait()
    for t, held in enumerate((xq, xk, xv)):
        loads[1 + t].wait()
        pick(t, held, mz)
    plane(mc)
    pl.semaphore_wait(mate, 1)
    plane(1 - mc)

    def pick_others(i, _):
        for t, held in enumerate((xq, xk, xv)):
            pick(t, held, lax.rem(mz + i, 4))
        return 0

    lax.fori_loop(1, 4, pick_others, 0)
    lax.fori_loop(1, 4, column, 0)
    pl.semaphore_wait(ready, 7)

    def far_half(i, _):
        z, x, y = anywhere(i)

        @pl.when((z != mz) & ((x != mx) | (y != my)))
        def _():
            send_half(z, x, y)

        return 0

    def first(i, _):
        send_part(0, *anywhere(i))
        return 0

    def second(i, _):
        send_part(1, *anywhere(i))
        return 0

    def anywhere(i):
        j = lax.rem(i * 29 + 32 * mc, 64)
        return lax.rem(mz + lax.rem(j, 4), 4), lax.rem(mx + lax.rem(lax.div(j, 4), 4), 4), lax.rem(my + lax.div(j, 16), 4)

    lax.fori_loop(0, 64, far_half, 0)
    lax.fori_loop(0, 64, first, 0)
    lax.fori_loop(0, 64, second, 0)
    for copy in loads[4:]:
        copy.wait()

    clip = plan[my_unit]
    live_frames = frames[clip]
    live_pos = height[clip] * width[clip]
    rows = recv.reshape(3, FRAMES, POS, D)
    key_bias = jnp.where(lax.broadcasted_iota(jnp.int32, (1, POS), 1) < live_pos, 0.0, -jnp.inf)

    ones = jnp.ones((POS, D), jnp.bfloat16)

    def attend(q, i, live):
        scores = lax.dot_general(q, rows[1, i], (((1,), (1,)), ((), ())), preferred_element_type=jnp.float32)
        scores = scores + key_bias
        top = jnp.max(scores, axis=-1, keepdims=True)
        weights = jnp.exp2((scores - top) * SCALE2)
        both = jnp.dot(
            weights.astype(jnp.bfloat16), jnp.concatenate([rows[2, i], ones], axis=1),
            preferred_element_type=jnp.float32,
        )
        mixed, total = both[:, :D], both[:, D:]
        on = jnp.where(my_first + i < live_frames, 1.0, 0.0)
        return (mixed * (live * on / total)).astype(jnp.bfloat16)

    gain = (gq[...] * gk[...]) * SCALE2
    T = FRAMES * BLOCK
    r_id = lax.broadcasted_iota(jnp.int32, (T, T), 0)
    c_id = lax.broadcasted_iota(jnp.int32, (T, T), 1)
    pair_on = (lax.rem(r_id, BLOCK) == lax.rem(c_id, BLOCK)) & (lax.div(c_id, BLOCK) < live_frames)
    pair_bias[...] = jnp.where(pair_on, 0.0, -jnp.inf)
    t_on = lax.div(lax.broadcasted_iota(jnp.int32, (T, 1), 0), BLOCK) < live_frames
    frame_on = jnp.where(t_on, 1.0, 0.0)

    def temporal(p0):
        xb = spat[:, pl.ds(p0, BLOCK), :].reshape(T, D)
        x = xb.astype(jnp.float32)
        inv = lax.rsqrt(jnp.sum(x * x, axis=-1, keepdims=True) * (1.0 / D) + 1e-6)
        y = x * inv * gain
        hi = y.astype(jnp.bfloat16)
        lo = (y - hi.astype(jnp.float32)).astype(jnp.bfloat16)
        scores = lax.dot_general(
            jnp.concatenate([xb, xb], axis=1), jnp.concatenate([hi, lo], axis=1),
            (((1,), (1,)), ((), ())), preferred_element_type=jnp.float32,
        )
        scores = scores + pair_bias[...]
        top = jnp.max(scores, axis=-1, keepdims=True)
        weights = jnp.exp2((scores - top) * inv)
        total = jnp.sum(weights, axis=-1, keepdims=True)
        mixed = jnp.dot(weights.astype(jnp.bfloat16), xb, preferred_element_type=jnp.float32)
        mixed = (mixed * (frame_on / total)).astype(jnp.bfloat16).astype(jnp.float32)
        sendbuf[:, pl.ds(p0, BLOCK), :] = (x + mixed).astype(jnp.bfloat16).reshape(FRAMES, BLOCK, D)

    head_lanes = pl.ds(pl.multiple_of(my_head * D, D), D)
    own_unit = my_unit == my_g

    def chunk(p0):
        def blocks(b, _):
            for k in range(TU):
                temporal(pl.multiple_of(p0 + (b * TU + k) * BLOCK, BLOCK))
            return 0

        lax.fori_loop(0, PC // BLOCK // TU, blocks, 0)
        span = pl.ds(p0, PC)

        def send_frame(f):
            src, dst = sendbuf.at[f, span], out.at[0, 0, span, head_lanes]
            here = (f == my_s) & own_unit

            @pl.when(jnp.logical_not(here))
            def _():
                pltpu.make_async_remote_copy(
                    src, dst, out_send, out_recv, device_id=(my_unit, f), device_id_type=MESH
                ).start()

            @pl.when(here)
            def _():
                pltpu.make_async_copy(src, dst, out_recv).start()

        for tier in TIERS:

            def send_tier(i, _, tier=tier):
                k = lax.rem(my_s + i, len(tier))
                f = tier[0]
                for n, frame in enumerate(tier):
                    f = jnp.where(k == n, frame, f)
                send_frame(f)
                return 0

            lax.fori_loop(0, len(tier), send_tier, 0)

    @pl.when(mc == 1)
    def _():
        wait_bytes(recv.at[:, pl.ds(0, HALF)], in_recv.at[0])
        live = jnp.where(lax.broadcasted_iota(jnp.int32, (POS, 1), 0) < live_pos, 1.0, 0.0)

        def group(b, _):
            for k in range(SU):
                i = b * SU + k
                spat[my_first + i] = attend(rows[0, i], i, live)
            return 0

        lax.fori_loop(0, HALF // SU, group, 0)

        half = lax.rem(my, 2)
        theirs = pl.ds(pl.multiple_of((1 - half) * (POS // 2), POS // 2), POS // 2)
        block = spat.at[pl.ds(my_first, HALF), theirs]
        copy = pltpu.make_async_remote_copy(
            block, block, pair_send, pair_recv, device_id=(my_g, my_s + 1 - 2 * half), device_id_type=MESH
        )
        copy.start()
        copy.wait()

        def half_chunk(k, _):
            chunk(pl.multiple_of(half * (POS // 2) + k * PC, PC))
            return 0

        lax.fori_loop(0, POS // 2 // PC, half_chunk, 0)
        wait_bytes(sendbuf.at[pl.ds(0, 15), pl.ds(0, POS // 2)], out_send)

    @pl.when(mc == 0)
    def _():
        live = jnp.where(lax.broadcasted_iota(jnp.int32, (POS, 1), 0) < live_pos, 1.0, 0.0)
        wait_bytes(recv.at[:, pl.ds(0, HALF)], in_recv.at[0])

        def first_frames(b, _):
            for k in range(SU):
                i = b * SU + k
                spat[i] = attend(rows[0, i], i, live)
            return 0

        lax.fori_loop(0, HALF // SU, first_frames, 0)

        wait_bytes(recv.at[:, pl.ds(0, HALF)], in_recv.at[1])

        def finish(c, _):
            p0 = pl.multiple_of(c * PC, PC)
            span = pl.ds(p0, PC)
            place = p0 + lax.broadcasted_iota(jnp.int32, (PC, 1), 0)
            on = jnp.where(place < live_pos, 1.0, 0.0)

            def last_frames(b, _):
                for k in range(LU):
                    i = HALF + b * LU + k
                    spat[i, span] = attend(rows[0, i, span], i, on)
                return 0

            lax.fori_loop(0, HALF // LU, last_frames, 0)
            chunk(p0)
            return 0

        lax.fori_loop(0, POS // PC, finish, 0)

        @pl.when(own_unit)
        def _():
            wait_bytes(sendbuf.at[pl.ds(0, 15)], out_send)

        @pl.when(jnp.logical_not(own_unit))
        def _():
            wait_bytes(sendbuf, out_send)

    sent(0, 1)
    sent(1, 0)
    sent(2, 0)
    wait_bytes(out, out_recv)


def on_device(
    queries, key_rows, values, query_gain, key_gain, frames_per_clip, latent_height, latent_width, clip_plan
):
    def by_head(x):
        return x.reshape(16, FRAMES, 2, HEADS, D).transpose(0, 1, 3, 2, 4)

    hbm = pl.BlockSpec(memory_space=pl.ANY)
    clips = pltpu.VMEM((16, FRAMES, HEADS, 2, D), jnp.bfloat16)
    counts = pltpu.SMEM((16,), jnp.int32)
    dma = pltpu.SemaphoreType.DMA
    return pl.pallas_call(
        kernel,
        out_shape=pltpu.VMEM((1, 1, POS, HEADS * D), jnp.bfloat16),
        in_specs=[hbm] * 9,
        out_specs=hbm,
        scratch_shapes=[
            pltpu.SMEM((8,), jnp.int32), counts, counts, counts,
            pltpu.VMEM((1, D), jnp.float32), pltpu.VMEM((1, D), jnp.float32),
            clips, clips, clips,
            pltpu.VMEM((8, 3, FRAMES, HEADS, 2, D), jnp.bfloat16),
            pltpu.VMEM((3, FRAMES, DEVS, 2, D), jnp.bfloat16),
            pltpu.VMEM((FRAMES, POS, D), jnp.bfloat16),
            pltpu.VMEM((FRAMES, POS, D), jnp.bfloat16),
            pltpu.VMEM((FRAMES * BLOCK, FRAMES * BLOCK), jnp.float32),
            dma((9,)), dma((3,)), dma((2,)), dma, dma, dma, dma,
            pltpu.SemaphoreType.REGULAR, pltpu.SemaphoreType.REGULAR,
        ],
        compiler_params=pltpu.CompilerParams(
            collective_id=0, has_side_effects=True, vmem_limit_bytes=VMEM_BYTES
        ),
        name="attend",
    )(
        clip_plan, frames_per_clip, latent_height, latent_width,
        by_head(queries), by_head(key_rows), by_head(values),
        query_gain.reshape(1, D), key_gain.reshape(1, D),
    )


def solution(mesh):
    split = P(None, None, ("grp", "sp"), None)
    return jax.shard_map(
        on_device,
        mesh=mesh,
        in_specs=(split, split, split, P(), P(), P(), P(), P(), P()),
        out_specs=P("grp", "sp", None, None),
        check_vma=False,
    )
```

```python
import functools
import math

import jax
import jax.numpy as jnp
from jax import lax
from jax.experimental import pallas as pl
from jax.experimental.pallas import tpu as pltpu
from jax.sharding import PartitionSpec as P

MESH = pl.DeviceIdType.MESH
D = 128
HEADS = 12
FRAMES = 16
POS = 256
DEVS = 128
HALF = FRAMES // 2
BLOCK = 16
PC = 128
VMEM_BYTES = 56 << 20
SU = 8
TIERS = ((0, 1, 3, 4, 12, 2, 8, 5), (7, 13, 15, 6, 9, 11, 14, 10))
LU = 8
TU = 8
SCALE2 = D**-0.5 * math.log2(math.e)


def unit_of(z, c, x, y):
    whole = x * 4 + y
    over = jnp.where(whole >= HEADS, 1, 0)
    group = jnp.where(c == 0, 2 * z + over, 2 * z + 1)
    head = jnp.where(c == 0, whole - HEADS * over, 4 + 2 * x + lax.div(y, 2))
    first_frame = jnp.where(c == 0, 0, HALF * lax.rem(y, 2))
    return group, head, first_frame


def kernel(
    plan_hbm, frames_hbm, height_hbm, width_hbm, q_hbm, k_hbm, v_hbm, gq_hbm, gk_hbm, out,
    plan, frames, height, width, gq, gk, xq, xk, xv, stage, recv, spat, sendbuf, pair_bias,
    x_sem, in_send, in_recv, pair_send, pair_recv, out_send, out_recv, ready, mate,
):
    my_g = lax.axis_index("grp")
    my_s = lax.axis_index("sp")
    me = my_g * 16 + my_s
    mz, mc = lax.div(my_g, 2), lax.rem(my_g, 2)
    mx, my = lax.div(my_s, 4), lax.rem(my_s, 4)
    my_unit, my_head, my_first = unit_of(mz, mc, mx, my)

    barrier = pltpu.get_barrier_semaphore()
    loads = [
        pltpu.make_async_copy(ref, held, x_sem.at[t])
        for t, (ref, held) in enumerate((
            (plan_hbm, plan), (q_hbm, xq), (k_hbm, xk), (v_hbm, xv), (frames_hbm, frames),
            (height_hbm, height), (width_hbm, width), (gq_hbm, gq), (gk_hbm, gk),
        ))
    ]

    def greet_grp(i, _):
        pl.semaphore_signal(barrier, 1, device_id=(lax.rem(my_g + i, 8), my_s), device_id_type=MESH)
        return 0

    def greet_sp(i, _):
        pl.semaphore_signal(barrier, 1, device_id=(my_g, lax.rem(my_s + i, 16)), device_id_type=MESH)
        return 0

    def greet_all(i, _):
        pl.semaphore_signal(ready, 1, device_id=(lax.rem(my_g + i, 8), my_s), device_id_type=MESH)
        return 0

    for copy in loads[:4]:
        copy.start()
    lax.fori_loop(1, 16, greet_sp, 0)
    lax.fori_loop(1, 8, greet_grp, 0)
    for copy in loads[4:]:
        copy.start()

    def wait_bytes(ref, sem):
        pltpu.make_async_copy(ref, ref, sem).wait()

    def sent(part, to_core):
        def of(count):
            wait_bytes(recv.at[:, pl.ds(0, HALF), pl.ds(0, count)], in_send.at[part])

        @pl.when(mc == to_core)
        def _():
            of(DEVS // 2 - 1)

        @pl.when(mc != to_core)
        def _():
            of(DEVS // 2)

    stage_rows = stage.reshape(8, 3, FRAMES * HEADS * 2, D)

    def pick(t, held, z):
        x_rows = held.reshape(16, FRAMES * HEADS * 2, D)
        for c in range(2):
            stage_rows[2 * z + c, t] = x_rows[plan[2 * z + c]]

    def send(src, dst, sem, arrival, z, c, x, y):
        here = (z == mz) & (c == mc) & (x == mx) & (y == my)

        @pl.when(jnp.logical_not(here))
        def _():
            pltpu.make_async_remote_copy(
                src, dst, in_send.at[sem], in_recv.at[arrival],
                device_id=(2 * z + c, 4 * x + y), device_id_type=MESH,
            ).start()

        @pl.when(here)
        def _():
            pltpu.make_async_copy(src, dst, in_recv.at[arrival]).start()

    def send_half(z, x, y):
        group, head, first = unit_of(z, 1, x, y)
        send(
            stage.at[group, :, pl.ds(first, HALF), head], recv.at[:, pl.ds(0, HALF), me], 0, 0, z, 1, x, y
        )

    def send_part(part, z, x, y):
        group, head, _ = unit_of(z, 0, x, y)
        span = pl.ds(part * HALF, HALF)
        send(stage.at[group, :, span, head], recv.at[:, span, me], 1 + part, part, z, 0, x, y)

    def near(i):
        return mz, lax.rem(mx + lax.div(i, 4), 4), lax.rem(my + lax.rem(i, 4), 4)

    def plane(c):
        @pl.when(c == 1)
        def _():
            def body(i, _):
                send_half(*near(lax.rem(i * 5, 16)))
                return 0

            lax.fori_loop(0, 16, body, 0)

        @pl.when(c == 0)
        def _():
            def body(i, _):
                pass
                return 0

            lax.fori_loop(0, 16, body, 0)

    def column(i, _):
        z = lax.rem(mz + i, 4)
        send_half(z, mx, my)
        return 0

    pl.semaphore_wait(barrier, 22)
    pl.semaphore_signal(mate, 1, device_id=(my_g + 1 - 2 * mc, my_s), device_id_type=MESH)
    lax.fori_loop(1, 8, greet_all, 0)
    loads[0].wait()
    for t, held in enumerate((xq, xk, xv)):
        loads[1 + t].wait()
        pick(t, held, mz)
    plane(mc)
    pl.semaphore_wait(mate, 1)
    plane(1 - mc)

    def pick_others(i, _):
        for t, held in enumerate((xq, xk, xv)):
            pick(t, held, lax.rem(mz + i, 4))
        return 0

    lax.fori_loop(1, 4, pick_others, 0)
    lax.fori_loop(1, 4, column, 0)
    pl.semaphore_wait(ready, 7)

    def far_half(i, _):
        z, x, y = anywhere(i)

        @pl.when((z != mz) & ((x != mx) | (y != my)))
        def _():
            send_half(z, x, y)

        return 0

    def first(i, _):
        send_part(0, *anywhere(i))
        return 0

    def second(i, _):
        send_part(1, *anywhere(i))
        return 0

    def anywhere(i):
        j = lax.rem(i * 29 + 32 * mc, 64)
        return lax.rem(mz + lax.rem(j, 4), 4), lax.rem(mx + lax.rem(lax.div(j, 4), 4), 4), lax.rem(my + lax.div(j, 16), 4)

    lax.fori_loop(0, 64, far_half, 0)
    lax.fori_loop(0, 64, first, 0)
    lax.fori_loop(0, 64, second, 0)
    for copy in loads[4:]:
        copy.wait()

    clip = plan[my_unit]
    live_frames = frames[clip]
    live_pos = height[clip] * width[clip]
    rows = recv.reshape(3, FRAMES, POS, D)
    key_bias = jnp.where(lax.broadcasted_iota(jnp.int32, (1, POS), 1) < live_pos, 0.0, -jnp.inf)

    ones = jnp.ones((POS, D), jnp.bfloat16)

    def attend(q, i, live):
        scores = lax.dot_general(q, rows[1, i], (((1,), (1,)), ((), ())), preferred_element_type=jnp.float32)
        scores = scores + key_bias
        top = jnp.max(scores, axis=-1, keepdims=True)
        weights = jnp.exp2((scores - top) * SCALE2)
        both = jnp.dot(
            weights.astype(jnp.bfloat16), jnp.concatenate([rows[2, i], ones], axis=1),
            preferred_element_type=jnp.float32,
        )
        mixed, total = both[:, :D], both[:, D:]
        on = jnp.where(my_first + i < live_frames, 1.0, 0.0)
        return (mixed * (live * on / total)).astype(jnp.bfloat16)

    gain = (gq[...] * gk[...]) * SCALE2
    T = FRAMES * BLOCK
    r_id = lax.broadcasted_iota(jnp.int32, (T, T), 0)
    c_id = lax.broadcasted_iota(jnp.int32, (T, T), 1)
    pair_on = (lax.rem(r_id, BLOCK) == lax.rem(c_id, BLOCK)) & (lax.div(c_id, BLOCK) < live_frames)
    pair_bias[...] = jnp.where(pair_on, 0.0, -jnp.inf)
    t_on = lax.div(lax.broadcasted_iota(jnp.int32, (T, 1), 0), BLOCK) < live_frames
    frame_on = jnp.where(t_on, 1.0, 0.0)

    def temporal(p0):
        xb = spat[:, pl.ds(p0, BLOCK), :].reshape(T, D)
        x = xb.astype(jnp.float32)
        inv = lax.rsqrt(jnp.sum(x * x, axis=-1, keepdims=True) * (1.0 / D) + 1e-6)
        y = x * inv * gain
        hi = y.astype(jnp.bfloat16)
        lo = (y - hi.astype(jnp.float32)).astype(jnp.bfloat16)
        scores = lax.dot_general(
            jnp.concatenate([xb, xb], axis=1), jnp.concatenate([hi, lo], axis=1),
            (((1,), (1,)), ((), ())), preferred_element_type=jnp.float32,
        )
        scores = scores + pair_bias[...]
        top = jnp.max(scores, axis=-1, keepdims=True)
        weights = jnp.exp2((scores - top) * inv)
        both = jnp.dot(
            weights.astype(jnp.bfloat16), jnp.concatenate([xb, ones], axis=1),
            preferred_element_type=jnp.float32,
        )
        mixed = (both[:, :D] * (frame_on / both[:, D:])).astype(jnp.bfloat16).astype(jnp.float32)
        sendbuf[:, pl.ds(p0, BLOCK), :] = (x + mixed).astype(jnp.bfloat16).reshape(FRAMES, BLOCK, D)

    head_lanes = pl.ds(pl.multiple_of(my_head * D, D), D)
    own_unit = my_unit == my_g

    def chunk(p0):
        def blocks(b, _):
            for k in range(TU):
                temporal(pl.multiple_of(p0 + (b * TU + k) * BLOCK, BLOCK))
            return 0

        lax.fori_loop(0, PC // BLOCK // TU, blocks, 0)
        span = pl.ds(p0, PC)

        def send_frame(f):
            src, dst = sendbuf.at[f, span], out.at[0, 0, span, head_lanes]
            here = (f == my_s) & own_unit

            @pl.when(jnp.logical_not(here))
            def _():
                pltpu.make_async_remote_copy(
                    src, dst, out_send, out_recv, device_id=(my_unit, f), device_id_type=MESH
                ).start()

            @pl.when(here)
            def _():
                pltpu.make_async_copy(src, dst, out_recv).start()

        for tier in TIERS:

            def send_tier(i, _, tier=tier):
                k = lax.rem(my_s + i, len(tier))
                f = tier[0]
                for n, frame in enumerate(tier):
                    f = jnp.where(k == n, frame, f)
                send_frame(f)
                return 0

            lax.fori_loop(0, len(tier), send_tier, 0)

    @pl.when(mc == 1)
    def _():
        wait_bytes(recv.at[:, pl.ds(0, HALF)], in_recv.at[0])
        live = jnp.where(lax.broadcasted_iota(jnp.int32, (POS, 1), 0) < live_pos, 1.0, 0.0)

        def group(b, _):
            for k in range(SU):
                i = b * SU + k
                spat[my_first + i] = attend(rows[0, i], i, live)
            return 0

        lax.fori_loop(0, HALF // SU, group, 0)

        half = lax.rem(my, 2)
        theirs = pl.ds(pl.multiple_of((1 - half) * (POS // 2), POS // 2), POS // 2)
        block = spat.at[pl.ds(my_first, HALF), theirs]
        copy = pltpu.make_async_remote_copy(
            block, block, pair_send, pair_recv, device_id=(my_g, my_s + 1 - 2 * half), device_id_type=MESH
        )
        copy.start()
        copy.wait()

        def half_chunk(k, _):
            chunk(pl.multiple_of(half * (POS // 2) + k * PC, PC))
            return 0

        lax.fori_loop(0, POS // 2 // PC, half_chunk, 0)
        wait_bytes(sendbuf.at[pl.ds(0, 15), pl.ds(0, POS // 2)], out_send)

    @pl.when(mc == 0)
    def _():
        live = jnp.where(lax.broadcasted_iota(jnp.int32, (POS, 1), 0) < live_pos, 1.0, 0.0)
        wait_bytes(recv.at[:, pl.ds(0, HALF)], in_recv.at[0])

        def first_frames(b, _):
            for k in range(SU):
                i = b * SU + k
                spat[i] = attend(rows[0, i], i, live)
            return 0

        lax.fori_loop(0, HALF // SU, first_frames, 0)

        wait_bytes(recv.at[:, pl.ds(0, HALF)], in_recv.at[1])

        def finish(c, _):
            p0 = pl.multiple_of(c * PC, PC)
            span = pl.ds(p0, PC)
            place = p0 + lax.broadcasted_iota(jnp.int32, (PC, 1), 0)
            on = jnp.where(place < live_pos, 1.0, 0.0)

            def last_frames(b, _):
                for k in range(LU):
                    i = HALF + b * LU + k
                    spat[i, span] = attend(rows[0, i, span], i, on)
                return 0

            lax.fori_loop(0, HALF // LU, last_frames, 0)
            chunk(p0)
            return 0

        lax.fori_loop(0, POS // PC, finish, 0)

        @pl.when(own_unit)
        def _():
            wait_bytes(sendbuf.at[pl.ds(0, 15)], out_send)

        @pl.when(jnp.logical_not(own_unit))
        def _():
            wait_bytes(sendbuf, out_send)

    sent(0, 1)
    sent(1, 0)
    sent(2, 0)
    wait_bytes(out, out_recv)


def on_device(
    queries, key_rows, values, query_gain, key_gain, frames_per_clip, latent_height, latent_width, clip_plan
):
    def by_head(x):
        return x.reshape(16, FRAMES, 2, HEADS, D).transpose(0, 1, 3, 2, 4)

    hbm = pl.BlockSpec(memory_space=pl.ANY)
    clips = pltpu.VMEM((16, FRAMES, HEADS, 2, D), jnp.bfloat16)
    counts = pltpu.SMEM((16,), jnp.int32)
    dma = pltpu.SemaphoreType.DMA
    return pl.pallas_call(
        kernel,
        out_shape=pltpu.VMEM((1, 1, POS, HEADS * D), jnp.bfloat16),
        in_specs=[hbm] * 9,
        out_specs=hbm,
        scratch_shapes=[
            pltpu.SMEM((8,), jnp.int32), counts, counts, counts,
            pltpu.VMEM((1, D), jnp.float32), pltpu.VMEM((1, D), jnp.float32),
            clips, clips, clips,
            pltpu.VMEM((8, 3, FRAMES, HEADS, 2, D), jnp.bfloat16),
            pltpu.VMEM((3, FRAMES, DEVS, 2, D), jnp.bfloat16),
            pltpu.VMEM((FRAMES, POS, D), jnp.bfloat16),
            pltpu.VMEM((FRAMES, POS, D), jnp.bfloat16),
            pltpu.VMEM((FRAMES * BLOCK, FRAMES * BLOCK), jnp.float32),
            dma((9,)), dma((3,)), dma((2,)), dma, dma, dma, dma,
            pltpu.SemaphoreType.REGULAR, pltpu.SemaphoreType.REGULAR,
        ],
        compiler_params=pltpu.CompilerParams(
            collective_id=0, has_side_effects=True, vmem_limit_bytes=VMEM_BYTES
        ),
        name="attend",
    )(
        clip_plan, frames_per_clip, latent_height, latent_width,
        by_head(queries), by_head(key_rows), by_head(values),
        query_gain.reshape(1, D), key_gain.reshape(1, D),
    )


def solution(mesh):
    split = P(None, None, ("grp", "sp"), None)
    return jax.shard_map(
        on_device,
        mesh=mesh,
        in_specs=(split, split, split, P(), P(), P(), P(), P(), P()),
        out_specs=P("grp", "sp", None, None),
        check_vma=False,
    )
```
